32 devices in a mesh: groups: 2 (over x), src: 16 (over z, y, core).
Axes of the slice: x: 2, y: 2, z: 4, core: 2. Of those that a mesh axis runs over, the one named last changes fastest.
Arguments:
- waveforms: bfloat16 [2048, 128, 256], P(None, 'src'), may hold values from -0.1875 to 0.1875
- onsets: int32 [4, 128], P('groups', 'src'), parts along dimension 0, may hold values from -256 to 255
- weights: int32 [4, 128], P('groups', 'src'), parts along dimension 0, may hold values from 1 to 13
- active: int32 [4, 128], P('groups', 'src'), parts along dimension 0, may hold values 0 or 1
- rates: bfloat16 [4, 128, 767], P('groups', 'src'), parts along dimension 0, may hold values from 0.099609375 to 2
- gauge_tiles: int32 [32], P('groups'), parts along dimension 0, may hold values from 0 to 15, each once
Outputs:
- forecast: float32 [2048, 4, 512], P('src', 'groups'), parts along dimension 1
The draws below stay inside these ranges and needn't reach their ends.
There are 2 independent parts, one for each index of `groups`. The reference program is written for one: setup_inputs(seed, part) draws one part's arguments, and reference() takes and returns one part's arrays. A program takes and returns all parts, laid end to end along the dimension named above; an argument that names none is the same for every part. Nothing has to cross between parts.
All inputs are finite; a program needn't handle non-finite values. No bound on the sum of `active` on one device may be relied on, other than what follows from the above.
Results may differ from the reference program's by a relative error of at most 0.0028.
Values may be sent and summed in bfloat16 or wider, within the bound.
A program may use at most 128 MiB of HBM per device.

```python
import math
import jax
import jax.numpy as jnp
from jax import lax

GAUGES = 2048
TAPS = 256
SAMPLES = 512
SCEN = 2
S_DEV = 8
GTILE = 128
SOURCES = 128
HIST = 767
N_SRC = 16


def draw_weights(key, part):
    index = jnp.arange(SOURCES, dtype=jnp.int32)
    upper = 2 + 12 * index // SOURCES
    values = jax.random.randint(key, (SCEN, SOURCES), 1, upper[None, :] + 1)
    row_index = jnp.arange(SCEN, dtype=jnp.int32)[:, None]
    values = jnp.where((row_index == 0) & (index[None, :] == SOURCES - 1), 13, values)
    values = jnp.where((row_index == 0) & (index[None, :] == 0), 1, values)
    return values.astype(jnp.int32)


def touch_ends(result, own_key, least, largest):
    spot = [jax.random.randint(jax.random.fold_in(own_key, axis), (), 0, length) for axis, length in enumerate(result.shape)]
    main_axis = result.shape.index(max(result.shape))
    beside = spot[:main_axis] + [(spot[main_axis] + 1) % result.shape[main_axis]] + spot[main_axis + 1:]
    return result.at[tuple(spot)].set(least).at[tuple(beside)].set(largest)


def steps_of(key, extent, cuts, least, high):
    def one(dim, blocks):
        steps = jax.random.uniform(jax.random.fold_in(jax.random.fold_in(key, 6), dim), (blocks,), jnp.float32, least / len(cuts), high / len(cuts))
        return jnp.repeat(jnp.exp(steps), extent[dim] // blocks).reshape((-1,) + (1,) * (len(extent) - dim - 1))

    level = one(*cuts[0])
    for cut in cuts[1:]:
        level = level * one(*cut)
    return level


def scatter_about(rng, shape, scale, most, split=(), kind=jnp.bfloat16):
    result = jax.random.normal(rng, shape, jnp.float32) * scale
    if len(split) > 0:
        result = steps_of(rng, shape, split, -0.22, 0.18) * result
    return jnp.clip(result, min=-most, max=most).astype(kind)


def setup_inputs(seed: int = 0, part: int = 0) -> dict:
    arg_keys = jax.random.split(jax.random.key(seed), 7)
    part_splits = jax.random.split(jax.random.fold_in(arg_keys[6], part), 7)
    waveforms = scatter_about(arg_keys[0], (GAUGES, SOURCES, TAPS), (4 * TAPS) ** -0.5, 0.1875, ((1, 16),))
    onsets = touch_ends(jax.random.randint(part_splits[1], (SCEN, SOURCES), 0 - TAPS, SAMPLES // 2), jax.random.fold_in(part_splits[1], 1), 0 - TAPS, (SAMPLES // 2) - 1).astype(jnp.int32)
    weights = draw_weights(jax.random.fold_in(jax.random.fold_in(arg_keys[6], part), 71), part)
    active = touch_ends((jax.random.randint(part_splits[3], (SCEN, SOURCES), 0, 4) < 3).astype(jnp.int32), jax.random.fold_in(part_splits[3], 1), 0, 1)
    rates = jnp.clip(jnp.exp(math.log(2.0) - 2.9996462 * jax.random.uniform(part_splits[4], (SCEN, SOURCES, HIST), jnp.float32) ** steps_of(part_splits[4], (SCEN, SOURCES, HIST), ((1, 16),), -0.2, 0.2)), 0.099609375, 2.0).astype(jnp.bfloat16)
    gauge_tiles = jax.random.permutation(part_splits[5], GAUGES // GTILE).astype(jnp.int32)
    return {"waveforms": waveforms, "onsets": onsets, "weights": weights, "active": active, "rates": rates, "gauge_tiles": gauge_tiles}


def rupture_matrix(onsets, weights, active, rates, count_t, count_k):
    sources = onsets.shape[1]
    scen = onsets.shape[0]
    amplitude = (weights * active).astype(jnp.float32)
    hist_index = lax.broadcasted_iota(jnp.int32, rates.shape, 2)
    live = (hist_index - (count_k - 1)) >= onsets[:, :, None]
    scaled = jnp.where(live, amplitude[:, :, None] * rates.astype(jnp.float32), jnp.float32(0.0)).astype(jnp.bfloat16)
    lag_index = lax.broadcasted_iota(jnp.int32, (count_k, count_t), 0)
    time_index = lax.broadcasted_iota(jnp.int32, (count_k, count_t), 1)
    position = time_index - lag_index + (count_k - 1)
    toeplitz = scaled[:, :, position]
    moment = jnp.transpose(toeplitz, (1, 2, 0, 3))
    return moment.reshape(sources * count_k, scen * count_t)


def reference(waveforms, onsets, weights, active, rates, gauge_tiles):
    def accumulate(index, total):
        start = (index * S_DEV).astype(jnp.int32)
        part_w = lax.dynamic_slice_in_dim(waveforms, start, S_DEV, 1).reshape(GAUGES, S_DEV * TAPS)
        moment = rupture_matrix(lax.dynamic_slice_in_dim(onsets, start, S_DEV, 1), lax.dynamic_slice_in_dim(weights, start, S_DEV, 1), lax.dynamic_slice_in_dim(active, start, S_DEV, 1), lax.dynamic_slice_in_dim(rates, start, S_DEV, 1), SAMPLES, TAPS)
        return total + jnp.dot(part_w, moment, preferred_element_type=jnp.float32).reshape(GAUGES, SCEN, SAMPLES)

    initial = jnp.zeros((GAUGES, SCEN, SAMPLES), jnp.float32)
    wave = lax.fori_loop(jnp.int32(0), jnp.int32(N_SRC), accumulate, initial)
    norm = jnp.sum(1 + weights * active, axis=1).astype(jnp.float32)
    wave = wave * (SOURCES / norm)[None, :, None]
    return jnp.take(wave.reshape(GAUGES // GTILE, GTILE, SCEN, SAMPLES), gauge_tiles, axis=0).reshape(GAUGES, SCEN, SAMPLES)
```

```python
import functools

import jax
import jax.numpy as jnp
from jax import lax
from jax.experimental import pallas as pl
from jax.experimental.pallas import tpu as pltpu
from jax.sharding import PartitionSpec as P

GTILE = 128
MESH = pl.DeviceIdType.MESH
F32 = jnp.float32
BF16 = jnp.bfloat16


def column(block):
    size = block.shape[1]
    eye = lax.broadcasted_iota(jnp.int32, (size, size), 0) == lax.broadcasted_iota(
        jnp.int32, (size, size), 1
    )
    wide = jnp.broadcast_to(block.astype(F32), (size, size))
    return jnp.sum(jnp.where(eye, wide, 0.0), axis=1, keepdims=True)


def kernel(
    width, scen, samples, taps,
    tiles_ref, onsets_ref, weights_ref, active_ref, rates_ref, w_hbm, out_ref,
    w_ref, scaled, moment, spread, lhs, keep,
    csend, crecv, ysend, yrecv, zsend, zrecv,
    ncs, ncr, nys, nyr, nzs, nzr,
    w_sem, cs_sem, cr_sem, ys_sem, yr_sem, zs_sem, zr_sem, n_ss, n_rs, nz_ss, nz_rs,
):
    line = width // 4
    steps = 2 * line
    rows = out_ref.shape[0]
    local = w_ref.shape[1]
    hist = rates_ref.shape[2]
    columns = scen * samples
    me = lax.axis_index("src")
    z = me // 4
    y = (me // 2) % 2
    core = me % 2
    mate = z * 4 + y * 2 + (1 - core)
    across = z * 4 + (1 - y) * 2 + core

    def peer(j):
        return ((z + 1 + j) % line) * 4 + y * 2 + core

    load = pltpu.make_async_copy(w_hbm, w_ref, w_sem)
    load.start()

    barrier = pltpu.get_barrier_semaphore()
    for other in (mate, across):
        pl.semaphore_signal(barrier, inc=1, device_id={"src": other}, device_id_type=MESH)

    @pl.loop(0, line - 1)
    def _(j):
        pl.semaphore_signal(barrier, inc=1, device_id={"src": peer(j)}, device_id_type=MESH)

    def remote(src, dst, ss, rs, to):
        return pltpu.make_async_remote_copy(
            src_ref=src, dst_ref=dst, send_sem=ss, recv_sem=rs,
            device_id={"src": to}, device_id_type=MESH,
        )

    def ccopy(q):
        return remote(csend.at[q], crecv.at[q], cs_sem.at[q], cr_sem.at[q], mate)

    def ycopy(i):
        return remote(ysend.at[i], yrecv.at[i], ys_sem.at[i], yr_sem.at[i], across)

    def zcopy(j):
        return remote(zsend.at[j], zrecv.at[j], zs_sem.at[j], zr_sem.at[j], peer(j))

    def nzcopy(j):
        return remote(nzs, nzr.at[j], nz_ss.at[j], nz_rs.at[j], peer(j))

    nc = remote(ncs, ncr, n_ss.at[0], n_rs.at[0], mate)
    ny = remote(nys, nyr, n_ss.at[1], n_rs.at[1], across)

    amount = weights_ref[...] * active_ref[...]
    ncs[...] = jnp.broadcast_to(
        jnp.sum((1 + amount).astype(F32), axis=1, keepdims=True), ncs.shape
    )
    scaled[...] = jnp.zeros_like(scaled)
    index = lax.broadcasted_iota(jnp.int32, (local, hist), 1) - (taps - 1)
    for c in range(scen):
        amplitude = column((weights_ref[c : c + 1, :] * active_ref[c : c + 1, :]))
        onset = column(onsets_ref[c : c + 1, :])
        live = index.astype(F32) >= onset
        value = jnp.where(live, amplitude * rates_ref[c].astype(F32), 0.0)
        scaled[c, :, :hist] = value

    padded = scaled.shape[2]
    half = taps // 2

    @pl.loop(0, local)
    def _(s):
        for c in range(scen):
            row = jnp.broadcast_to(scaled[c, pl.ds(s, 1), :], (half, padded))
            turned = pltpu.roll(
                row, shift=padded - (half - 1), axis=1, stride=1, stride_axis=0
            ).astype(BF16)
            base = pl.multiple_of(s * taps, taps)
            where = slice(c * samples, (c + 1) * samples)
            moment[pl.ds(base, half), where] = turned[:, half : half + samples]
            moment[pl.ds(pl.multiple_of(base + half, half), half), where] = turned[:, :samples]

    load.wait()
    pl.semaphore_wait(barrier, 2 + line - 1)
    nc.start()

    def compute(q):
        flip = q // line
        i = q % line
        zz = (z + 1 + i) % line
        yy = (1 - y) * (1 - flip) + y * flip
        for part in range(2):
            cc = (1 - core) * (1 - part) + core * part
            dest = (zz * 4 + yy * 2 + cc) * rows
            gauge = tiles_ref[dest // GTILE] * GTILE + dest % GTILE
            for n in range(taps // 128):
                block = w_ref[pl.ds(gauge, rows), :, n * 128 : (n + 1) * 128]
                spread[n] = block.astype(F32).reshape(rows * local, 128)
            for n in range(taps // 128):
                for s in range(local):
                    lhs[part * rows : (part + 1) * rows, s * taps + n * 128 : s * taps + (n + 1) * 128] = spread[
                        n, pl.ds(s, rows, stride=local), :
                    ].astype(BF16)

        @pl.loop(0, columns // 256)
        def _(n):
            cols = pl.ds(pl.multiple_of(n * 256, 256), 256)
            total = jnp.dot(lhs[...], moment[:, cols], preferred_element_type=F32)
            csend[q, :, cols] = total[:rows].astype(BF16)
            keep[q, :, cols] = total[rows:]

        ccopy(q).start()

    def first(i):
        ccopy(i).wait_recv()
        ysend[i] = (keep[i] + crecv[i].astype(F32)).astype(BF16)
        ycopy(i).start()

        @pl.when(i == 0)
        def _():
            nc.wait()
            nys[...] = ncs[...] + ncr[...]
            ny.start()

    def summed(i):
        ccopy(line + i).wait_recv()
        ycopy(i).wait_recv()
        return keep[line + i] + crecv[line + i].astype(F32) + yrecv[i].astype(F32)

    def second(i):
        zsend[i] = summed(i).astype(BF16)
        zcopy(i).start()

    @pl.loop(0, steps)
    def _(q):
        compute(q)

        @pl.when((q >= 1) & (q <= line))
        def _():
            first(q - 1)

        @pl.when(q == line)
        def _():
            ny.wait()
            nzs[...] = nys[...] + nyr[...]

            @pl.loop(0, line - 1)
            def _(j):
                nzcopy(j).start()

        @pl.when(q >= line + 1)
        def _():
            second(q - line - 1)

    keep[0] = summed(line - 1)

    @pl.loop(0, line - 1)
    def _(j):
        nzcopy(j).wait_recv()
        zcopy(j).wait_recv()

    def add_norm(j, norm):
        return norm + nzr[j]

    norm = lax.fori_loop(0, line - 1, add_norm, nzs[...])
    scale = jnp.full_like(norm, local * width) / norm

    @pl.loop(0, line - 2)
    def _(j):
        keep[0] += zrecv[j].astype(F32)

    for c in range(scen):
        where = slice(c * samples, (c + 1) * samples)
        out_ref[:, where] = (keep[0, :, where] + zrecv[line - 2, :, where].astype(F32)) * scale[
            c : c + 1, :1
        ]

    @pl.loop(0, steps)
    def _(q):
        ccopy(q).wait_send()

    @pl.loop(0, line)
    def _(i):
        ycopy(i).wait_send()

    @pl.loop(0, line - 1)
    def _(j):
        zcopy(j).wait_send()
        nzcopy(j).wait_send()


def per_device(waveforms, onsets, weights, active, rates, gauge_tiles):
    gauges, local, taps = waveforms.shape
    scen, _, hist = rates.shape
    samples = hist - taps + 1
    width = lax.axis_size("src")
    line = width // 4
    rows = gauges // width
    columns = scen * samples
    vmem = pl.BlockSpec(memory_space=pltpu.VMEM)
    dma = pltpu.SemaphoreType.DMA
    out = pl.pallas_call(
        functools.partial(kernel, width, scen, samples, taps),
        out_shape=jax.ShapeDtypeStruct((rows, columns), F32),
        in_specs=[pl.BlockSpec(memory_space=pltpu.SMEM)] + [vmem] * 4 + [pl.BlockSpec(memory_space=pl.ANY)],
        out_specs=vmem,
        scratch_shapes=[
            pltpu.VMEM((gauges, local, taps), BF16),
            pltpu.VMEM((scen, local, hist + 1), F32),
            pltpu.VMEM((local * taps, columns), BF16),
            pltpu.VMEM((taps // 128, rows * local, 128), F32),
            pltpu.VMEM((2 * rows, local * taps), BF16),
            pltpu.VMEM((2 * line, rows, columns), F32),
            pltpu.VMEM((2 * line, rows, columns), BF16),
            pltpu.VMEM((2 * line, rows, columns), BF16),
            pltpu.VMEM((line, rows, columns), BF16),
            pltpu.VMEM((line, rows, columns), BF16),
            pltpu.VMEM((line - 1, rows, columns), BF16),
            pltpu.VMEM((line - 1, rows, columns), BF16),
            pltpu.VMEM((scen, 128), F32),
            pltpu.VMEM((scen, 128), F32),
            pltpu.VMEM((scen, 128), F32),
            pltpu.VMEM((scen, 128), F32),
            pltpu.VMEM((scen, 128), F32),
            pltpu.VMEM((line - 1, scen, 128), F32),
            dma,
            dma((2 * line,)),
            dma((2 * line,)),
            dma((line,)),
            dma((line,)),
            dma((line - 1,)),
            dma((line - 1,)),
            dma((2,)),
            dma((2,)),
            dma((line - 1,)),
            dma((line - 1,)),
        ],
        compiler_params=pltpu.CompilerParams(
            collective_id=0, has_side_effects=True, vmem_limit_bytes=48 * 2**20
        ),
        cost_estimate=pl.CostEstimate(
            flops=2 * gauges * local * taps * columns,
            bytes_accessed=gauges * local * taps * 2,
            transcendentals=0,
        ),
    )(gauge_tiles, onsets, weights, active, rates, waveforms)
    return out.reshape(rows, scen, samples)


def solution(mesh):
    placed = (
        P(None, "src", None),
        P("groups", "src"),
        P("groups", "src"),
        P("groups", "src"),
        P("groups", "src", None),
        P("groups"),
    )
    return jax.shard_map(
        per_device, mesh=mesh, in_specs=placed, out_specs=P("src", "groups", None), check_vma=False
    )
```

```python
import functools

import jax
import jax.numpy as jnp
from jax import lax
from jax.experimental import pallas as pl
from jax.experimental.pallas import tpu as pltpu
from jax.sharding import PartitionSpec as P

GTILE = 128
MESH = pl.DeviceIdType.MESH
F32 = jnp.float32
BF16 = jnp.bfloat16


def column(block):
    size = block.shape[1]
    eye = lax.broadcasted_iota(jnp.int32, (size, size), 0) == lax.broadcasted_iota(
        jnp.int32, (size, size), 1
    )
    wide = jnp.broadcast_to(block.astype(F32), (size, size))
    return jnp.sum(jnp.where(eye, wide, 0.0), axis=1, keepdims=True)


def kernel(
    width, scen, samples, taps,
    tiles_hbm, onsets_hbm, weights_hbm, active_hbm, rates_hbm, w_hbm, out_ref,
    tiles_ref, onsets_ref, weights_ref, active_ref, rates_ref, small_sem,
    w_ref, scaled, moment, spread, lhs, keep,
    csend, crecv, ysend, yrecv, zsend, zrecv,
    ncs, ncr, nys, nyr, nzs, nzr,
    w_sem, cs_sem, cr_sem, ys_sem, yr_sem, zs_sem, zr_sem, n_ss, n_rs, nz_ss, nz_rs,
):
    line = width // 4
    steps = 2 * line
    rows = out_ref.shape[0]
    local = w_ref.shape[1]
    hist = rates_ref.shape[2]
    columns = scen * samples
    me = lax.axis_index("src")
    z = me // 4
    y = (me // 2) % 2
    core = me % 2
    mate = z * 4 + y * 2 + (1 - core)
    across = z * 4 + (1 - y) * 2 + core

    def peer(j):
        return ((z + 1 + j) % line) * 4 + y * 2 + core

    small = [
        pltpu.make_async_copy(src, dst, small_sem.at[n])
        for n, (src, dst) in enumerate(
            (
                (rates_hbm, rates_ref),
                (onsets_hbm, onsets_ref),
                (weights_hbm, weights_ref),
                (active_hbm, active_ref),
                (tiles_hbm, tiles_ref),
            )
        )
    ]
    for copy in small:
        copy.start()
    load = pltpu.make_async_copy(w_hbm, w_ref, w_sem)
    load.start()

    barrier = pltpu.get_barrier_semaphore()
    for other in (mate, across):
        pl.semaphore_signal(barrier, inc=1, device_id={"src": other}, device_id_type=MESH)

    @pl.loop(0, line - 1)
    def _(j):
        pl.semaphore_signal(barrier, inc=1, device_id={"src": peer(j)}, device_id_type=MESH)

    def remote(src, dst, ss, rs, to):
        return pltpu.make_async_remote_copy(
            src_ref=src, dst_ref=dst, send_sem=ss, recv_sem=rs,
            device_id={"src": to}, device_id_type=MESH,
        )

    def ccopy(q):
        return remote(csend.at[q], crecv.at[q], cs_sem.at[q], cr_sem.at[q], mate)

    def ycopy(i):
        return remote(ysend.at[i], yrecv.at[i], ys_sem.at[i], yr_sem.at[i], across)

    def zcopy(j):
        return remote(zsend.at[j], zrecv.at[j], zs_sem.at[j], zr_sem.at[j], peer(j))

    def nzcopy(j):
        return remote(nzs, nzr.at[j], nz_ss.at[j], nz_rs.at[j], peer(j))

    nc = remote(ncs, ncr, n_ss.at[0], n_rs.at[0], mate)
    ny = remote(nys, nyr, n_ss.at[1], n_rs.at[1], across)

    for copy in small:
        copy.wait()
    amount = weights_ref[...] * active_ref[...]
    ncs[...] = jnp.broadcast_to(
        jnp.sum((1 + amount).astype(F32), axis=1, keepdims=True), ncs.shape
    )
    scaled[...] = jnp.zeros_like(scaled)
    index = lax.broadcasted_iota(jnp.int32, (local, hist), 1) - (taps - 1)
    for c in range(scen):
        amplitude = column((weights_ref[c : c + 1, :] * active_ref[c : c + 1, :]))
        onset = column(onsets_ref[c : c + 1, :])
        live = index.astype(F32) >= onset
        value = jnp.where(live, amplitude * rates_ref[c].astype(F32), 0.0)
        scaled[c, :, :hist] = value

    padded = scaled.shape[2]
    half = taps // 2

    @pl.loop(0, local)
    def _(s):
        for c in range(scen):
            row = jnp.broadcast_to(scaled[c, pl.ds(s, 1), :], (8, padded))
            eight = pltpu.roll(row, shift=padded - (half - 1), axis=1, stride=1, stride_axis=0)
            turned = jnp.concatenate(
                [eight] + [pltpu.roll(eight, shift=8 * n, axis=1) for n in range(1, half // 8)],
                axis=0,
            ).astype(BF16)
            base = pl.multiple_of(s * taps, taps)
            where = slice(c * samples, (c + 1) * samples)
            moment[pl.ds(base, half), where] = turned[:, half : half + samples]
            moment[pl.ds(pl.multiple_of(base + half, half), half), where] = turned[:, :samples]

    load.wait()
    pl.semaphore_wait(barrier, 2 + line - 1)
    nc.start()

    def compute(flip, i):
        q = flip * line + i
        zz = (z + 1 + i) % line
        yy = (1 - y) * (1 - flip) + y * flip
        for part in range(2):
            cc = (1 - core) * (1 - part) + core * part
            dest = (zz * 4 + yy * 2 + cc) * rows
            gauge = tiles_ref[dest // GTILE] * GTILE + dest % GTILE
            for n in range(taps // 128):
                block = w_ref[pl.ds(gauge, rows), :, n * 128 : (n + 1) * 128]
                spread[n] = block.astype(F32).reshape(rows * local, 128)
            for n in range(taps // 128):
                for s in range(local):
                    lhs[part * rows : (part + 1) * rows, s * taps + n * 128 : s * taps + (n + 1) * 128] = spread[
                        n, pl.ds(s, rows, stride=local), :
                    ].astype(BF16)

        @pl.loop(0, columns // 256)
        def _(n):
            cols = pl.ds(pl.multiple_of(n * 256, 256), 256)
            total = jnp.dot(lhs[...], moment[:, cols], preferred_element_type=F32)
            csend[q, :, cols] = total[:rows].astype(BF16)
            keep[q, :, cols] = total[rows:]

        ccopy(q).start()

    def first(i):
        ccopy(i).wait_recv()
        ysend[i] = (keep[i] + crecv[i].astype(F32)).astype(BF16)

        @pl.when(i > 0)
        def _():
            ycopy(i - 1).wait_send()

        ycopy(i).start()

        @pl.when(i == 0)
        def _():
            nc.wait()
            nys[...] = ncs[...] + ncr[...]
            ny.start()

    def summed(i):
        ccopy(line + i).wait_recv()
        ycopy(i).wait_recv()
        return keep[line + i] + crecv[line + i].astype(F32) + yrecv[i].astype(F32)

    def second(i):
        zsend[i] = summed(i).astype(BF16)
        zcopy(i).start()

    @pl.loop(0, steps + 2)
    def _(p):
        flip = p % 2
        i = p // 2 - flip

        @pl.when((i >= 0) & (i < line))
        def _():
            compute(flip, i)

        @pl.when((flip == 0) & (i >= 1))
        def _():
            first(i - 1)

        @pl.when((flip == 0) & (i >= 2))
        def _():
            second(i - 2)

        @pl.when((flip == 0) & (i == 2))
        def _():
            ny.wait()
            nzs[...] = nys[...] + nyr[...]

            @pl.loop(0, line - 1)
            def _(j):
                nzcopy(j).start()

    keep[0] = summed(line - 1)

    @pl.loop(0, line - 1)
    def _(j):
        nzcopy(j).wait_recv()
        zcopy(j).wait_recv()

    def add_norm(j, norm):
        return norm + nzr[j]

    norm = lax.fori_loop(0, line - 1, add_norm, nzs[...])
    scale = jnp.full_like(norm, local * width) / norm

    @pl.loop(0, line - 2)
    def _(j):
        keep[0] += zrecv[j].astype(F32)

    for c in range(scen):
        where = slice(c * samples, (c + 1) * samples)
        out_ref[:, where] = (keep[0, :, where] + zrecv[line - 2, :, where].astype(F32)) * scale[
            c : c + 1, :1
        ]

    @pl.loop(0, steps)
    def _(q):
        ccopy(q).wait_send()

    ycopy(line - 1).wait_send()

    @pl.loop(0, line - 1)
    def _(j):
        zcopy(j).wait_send()
        nzcopy(j).wait_send()


def per_device(waveforms, onsets, weights, active, rates, gauge_tiles):
    gauges, local, taps = waveforms.shape
    scen, _, hist = rates.shape
    samples = hist - taps + 1
    width = lax.axis_size("src")
    line = width // 4
    rows = gauges // width
    columns = scen * samples
    vmem = pl.BlockSpec(memory_space=pltpu.VMEM)
    dma = pltpu.SemaphoreType.DMA
    out = pl.pallas_call(
        functools.partial(kernel, width, scen, samples, taps),
        out_shape=jax.ShapeDtypeStruct((rows, columns), F32),
        in_specs=[pl.BlockSpec(memory_space=pltpu.HBM)] * 6,
        out_specs=vmem,
        scratch_shapes=[
            pltpu.SMEM(gauge_tiles.shape, jnp.int32),
            pltpu.VMEM(onsets.shape, jnp.int32),
            pltpu.VMEM(weights.shape, jnp.int32),
            pltpu.VMEM(active.shape, jnp.int32),
            pltpu.VMEM(rates.shape, BF16),
            dma((5,)),
            pltpu.VMEM((gauges, local, taps), BF16),
            pltpu.VMEM((scen, local, hist + 1), F32),
            pltpu.VMEM((local * taps, columns), BF16),
            pltpu.VMEM((taps // 128, rows * local, 128), F32),
            pltpu.VMEM((2 * rows, local * taps), BF16),
            pltpu.VMEM((2 * line, rows, columns), F32),
            pltpu.VMEM((2 * line, rows, columns), BF16),
            pltpu.VMEM((2 * line, rows, columns), BF16),
            pltpu.VMEM((line, rows, columns), BF16),
            pltpu.VMEM((line, rows, columns), BF16),
            pltpu.VMEM((line - 1, rows, columns), BF16),
            pltpu.VMEM((line - 1, rows, columns), BF16),
            pltpu.VMEM((scen, 128), F32),
            pltpu.VMEM((scen, 128), F32),
            pltpu.VMEM((scen, 128), F32),
            pltpu.VMEM((scen, 128), F32),
            pltpu.VMEM((scen, 128), F32),
            pltpu.VMEM((line - 1, scen, 128), F32),
            dma,
            dma((2 * line,)),
            dma((2 * line,)),
            dma((line,)),
            dma((line,)),
            dma((line - 1,)),
            dma((line - 1,)),
            dma((2,)),
            dma((2,)),
            dma((line - 1,)),
            dma((line - 1,)),
        ],
        compiler_params=pltpu.CompilerParams(
            collective_id=0, has_side_effects=True, vmem_limit_bytes=63 * 2**20
        ),
        cost_estimate=pl.CostEstimate(
            flops=2 * gauges * local * taps * columns,
            bytes_accessed=gauges * local * taps * 2,
            transcendentals=0,
        ),
    )(gauge_tiles, onsets, weights, active, rates, waveforms)
    return out.reshape(rows, scen, samples)


def solution(mesh):
    placed = (
        P(None, "src", None),
        P("groups", "src"),
        P("groups", "src"),
        P("groups", "src"),
        P("groups", "src", None),
        P("groups"),
    )
    return jax.shard_map(
        per_device, mesh=mesh, in_specs=placed, out_specs=P("src", "groups", None), check_vma=False
    )
```

```python
import functools

import jax
import jax.numpy as jnp
from jax import lax
from jax.experimental import pallas as pl
from jax.experimental.pallas import tpu as pltpu
from jax.sharding import PartitionSpec as P

GTILE = 128
MESH = pl.DeviceIdType.MESH
F32 = jnp.float32
BF16 = jnp.bfloat16


def column(block):
    size = block.shape[1]
    eye = lax.broadcasted_iota(jnp.int32, (size, size), 0) == lax.broadcasted_iota(
        jnp.int32, (size, size), 1
    )
    wide = jnp.broadcast_to(block.astype(F32), (size, size))
    return jnp.sum(jnp.where(eye, wide, 0.0), axis=1, keepdims=True)


def kernel(
    width, scen, samples, taps,
    tiles_hbm, onsets_hbm, weights_hbm, active_hbm, rates_hbm, w_hbm, out_ref,
    tiles_ref, onsets_ref, weights_ref, active_ref, rates_ref, small_sem,
    w_ref, scaled, moment, spread, lhs, keep,
    csend, crecv, ysend, yrecv, zsend, zrecv,
    ncs, ncr, nys, nyr, nzs, nzr,
    w_sem, cs_sem, cr_sem, ys_sem, yr_sem, zs_sem, zr_sem, n_ss, n_rs, nz_ss, nz_rs,
):
    line = width // 4
    steps = 2 * line
    rows = out_ref.shape[0]
    local = w_ref.shape[1]
    hist = rates_ref.shape[2]
    columns = scen * samples
    me = lax.axis_index("src")
    z = me // 4
    y = (me // 2) % 2
    core = me % 2
    mate = z * 4 + y * 2 + (1 - core)
    across = z * 4 + (1 - y) * 2 + core

    def stage(i):
        ahead = (1 + (i + 1) % (line - 1)) * (1 - i // (line - 1))
        return (z + ahead) % line

    def peer(j):
        return stage(j) * 4 + y * 2 + core

    small = [
        pltpu.make_async_copy(src, dst, small_sem.at[n])
        for n, (src, dst) in enumerate(
            (
                (rates_hbm, rates_ref),
                (onsets_hbm, onsets_ref),
                (weights_hbm, weights_ref),
                (active_hbm, active_ref),
                (tiles_hbm, tiles_ref),
            )
        )
    ]
    for copy in small:
        copy.start()
    load = pltpu.make_async_copy(w_hbm, w_ref, w_sem)
    load.start()

    barrier = pltpu.get_barrier_semaphore()
    for other in (mate, across):
        pl.semaphore_signal(barrier, inc=1, device_id={"src": other}, device_id_type=MESH)

    @pl.loop(0, line - 1)
    def _(j):
        pl.semaphore_signal(barrier, inc=1, device_id={"src": peer(j)}, device_id_type=MESH)

    def remote(src, dst, ss, rs, to):
        return pltpu.make_async_remote_copy(
            src_ref=src, dst_ref=dst, send_sem=ss, recv_sem=rs,
            device_id={"src": to}, device_id_type=MESH,
        )

    def ccopy(q):
        return remote(csend.at[q], crecv.at[q], cs_sem.at[q], cr_sem.at[q], mate)

    def ycopy(i):
        return remote(ysend.at[i], yrecv.at[i], ys_sem.at[i], yr_sem.at[i], across)

    def zcopy(j):
        return remote(zsend.at[j], zrecv.at[j], zs_sem.at[j], zr_sem.at[j], peer(j // scen))

    def nzcopy(j):
        return remote(nzs, nzr.at[j], nz_ss.at[j], nz_rs.at[j], peer(j))

    nc = remote(ncs, ncr, n_ss.at[0], n_rs.at[0], mate)
    ny = remote(nys, nyr, n_ss.at[1], n_rs.at[1], across)

    for copy in small:
        copy.wait()
    amount = weights_ref[...] * active_ref[...]
    ncs[...] = jnp.broadcast_to(
        jnp.sum((1 + amount).astype(F32), axis=1, keepdims=True), ncs.shape
    )
    scaled[...] = jnp.zeros_like(scaled)
    index = lax.broadcasted_iota(jnp.int32, (local, hist), 1) - (taps - 1)
    for c in range(scen):
        amplitude = column((weights_ref[c : c + 1, :] * active_ref[c : c + 1, :]))
        onset = column(onsets_ref[c : c + 1, :])
        live = index.astype(F32) >= onset
        value = jnp.where(live, amplitude * rates_ref[c].astype(F32), 0.0)
        scaled[c, :, :hist] = value

    padded = scaled.shape[2]
    half = taps // 2

    @pl.loop(0, local)
    def _(s):
        for c in range(scen):
            row = jnp.broadcast_to(scaled[c, pl.ds(s, 1), :], (8, padded))
            eight = pltpu.roll(row, shift=padded - (half - 1), axis=1, stride=1, stride_axis=0)
            turned = jnp.concatenate(
                [eight] + [pltpu.roll(eight, shift=8 * n, axis=1) for n in range(1, half // 8)],
                axis=0,
            ).astype(BF16)
            base = pl.multiple_of(s * taps, taps)
            where = slice(c * samples, (c + 1) * samples)
            moment[pl.ds(base, half), where] = turned[:, half : half + samples]
            moment[pl.ds(pl.multiple_of(base + half, half), half), where] = turned[:, :samples]

    load.wait()
    pl.semaphore_wait(barrier, 2 + line - 1)
    nc.start()

    def compute(flip, i):
        q = flip * line + i
        zz = stage(i)
        yy = (1 - y) * (1 - flip) + y * flip
        for part in range(2):
            cc = (1 - core) * (1 - part) + core * part
            dest = (zz * 4 + yy * 2 + cc) * rows
            gauge = tiles_ref[dest // GTILE] * GTILE + dest % GTILE
            for n in range(taps // 128):
                block = w_ref[pl.ds(gauge, rows), :, n * 128 : (n + 1) * 128]
                spread[n] = block.astype(F32).reshape(rows * local, 128)
            for n in range(taps // 128):
                for s in range(local):
                    lhs[part * rows : (part + 1) * rows, s * taps + n * 128 : s * taps + (n + 1) * 128] = spread[
                        n, pl.ds(s, rows, stride=local), :
                    ].astype(BF16)

        for c in range(scen):
            k = q * scen + c

            @pl.loop(0, samples // 256)
            def _(n):
                cols = pl.ds(pl.multiple_of(n * 256, 256), 256)
                wide = pl.ds(pl.multiple_of(c * samples + n * 256, 256), 256)
                total = jnp.dot(lhs[...], moment[:, wide], preferred_element_type=F32)
                csend[k, :, cols] = total[:rows].astype(BF16)
                keep[k, :, cols] = total[rows:]

            ccopy(k).start()

    def first(i, c):
        k = i * scen + c
        ccopy(k).wait_recv()
        ysend[k] = (keep[k] + crecv[k].astype(F32)).astype(BF16)

        @pl.when(i > 0)
        def _():
            ycopy(k - scen).wait_send()

        ycopy(k).start()

    def summed(i, c):
        k = i * scen + c
        far = line * scen + k
        ccopy(far).wait_recv()
        ycopy(k).wait_recv()
        return keep[far] + crecv[far].astype(F32) + yrecv[k].astype(F32)

    def second(i, c):
        k = i * scen + c
        zsend[k] = summed(i, c).astype(BF16)
        zcopy(k).start()

    @pl.loop(0, steps + 2)
    def _(p):
        flip = p % 2
        i = p // 2 - flip

        @pl.when((i >= 0) & (i < line))
        def _():
            compute(flip, i)

        for c in range(scen):

            @pl.when((flip == 0) & (i >= 1))
            def _():
                first(i - 1, c)

            @pl.when((flip == 0) & (i >= 2))
            def _():
                second(i - 2, c)

        @pl.when((flip == 0) & (i == 1))
        def _():
            nc.wait()
            nys[...] = ncs[...] + ncr[...]
            ny.start()

        @pl.when((flip == 0) & (i == 2))
        def _():
            ny.wait()
            nzs[...] = nys[...] + nyr[...]

            @pl.loop(0, line - 1)
            def _(j):
                nzcopy(j).start()

    for c in range(scen):
        keep[c] = summed(line - 1, c)

    @pl.loop(0, line - 1)
    def _(j):
        nzcopy(j).wait_recv()

    def add_norm(j, norm):
        return norm + nzr[j]

    norm = lax.fori_loop(0, line - 1, add_norm, nzs[...])
    scale = jnp.full_like(norm, local * width) / norm

    @pl.loop(0, line - 2)
    def _(j):
        for c in range(scen):
            k = j * scen + c
            zcopy(k).wait_recv()
            keep[c] += zrecv[k].astype(F32)

    for c in range(scen):
        k = (line - 2) * scen + c
        zcopy(k).wait_recv()
        out_ref[:, c * samples : (c + 1) * samples] = (
            keep[c] + zrecv[k].astype(F32)
        ) * scale[c : c + 1, :1]

    @pl.loop(0, steps * scen)
    def _(q):
        ccopy(q).wait_send()

    for c in range(scen):
        ycopy((line - 1) * scen + c).wait_send()

    @pl.loop(0, (line - 1) * scen)
    def _(k):
        zcopy(k).wait_send()

    @pl.loop(0, line - 1)
    def _(j):
        nzcopy(j).wait_send()


def per_device(waveforms, onsets, weights, active, rates, gauge_tiles):
    gauges, local, taps = waveforms.shape
    scen, _, hist = rates.shape
    samples = hist - taps + 1
    width = lax.axis_size("src")
    line = width // 4
    rows = gauges // width
    columns = scen * samples
    vmem = pl.BlockSpec(memory_space=pltpu.VMEM)
    dma = pltpu.SemaphoreType.DMA
    out = pl.pallas_call(
        functools.partial(kernel, width, scen, samples, taps),
        out_shape=pltpu.VMEM((rows, columns), F32),
        in_specs=[pl.BlockSpec(memory_space=pltpu.HBM)] * 6,
        out_specs=vmem,
        scratch_shapes=[
            pltpu.SMEM(gauge_tiles.shape, jnp.int32),
            pltpu.VMEM(onsets.shape, jnp.int32),
            pltpu.VMEM(weights.shape, jnp.int32),
            pltpu.VMEM(active.shape, jnp.int32),
            pltpu.VMEM(rates.shape, BF16),
            dma((5,)),
            pltpu.VMEM((gauges, local, taps), BF16),
            pltpu.VMEM((scen, local, hist + 1), F32),
            pltpu.VMEM((local * taps, columns), BF16),
            pltpu.VMEM((taps // 128, rows * local, 128), F32),
            pltpu.VMEM((2 * rows, local * taps), BF16),
            pltpu.VMEM((2 * line * scen, rows, samples), F32),
            pltpu.VMEM((2 * line * scen, rows, samples), BF16),
            pltpu.VMEM((2 * line * scen, rows, samples), BF16),
            pltpu.VMEM((line * scen, rows, samples), BF16),
            pltpu.VMEM((line * scen, rows, samples), BF16),
            pltpu.VMEM(((line - 1) * scen, rows, samples), BF16),
            pltpu.VMEM(((line - 1) * scen, rows, samples), BF16),
            pltpu.VMEM((scen, 128), F32),
            pltpu.VMEM((scen, 128), F32),
            pltpu.VMEM((scen, 128), F32),
            pltpu.VMEM((scen, 128), F32),
            pltpu.VMEM((scen, 128), F32),
            pltpu.VMEM((line - 1, scen, 128), F32),
            dma,
            dma((2 * line * scen,)),
            dma((2 * line * scen,)),
            dma((line * scen,)),
            dma((line * scen,)),
            dma(((line - 1) * scen,)),
            dma(((line - 1) * scen,)),
            dma((2,)),
            dma((2,)),
            dma((line - 1,)),
            dma((line - 1,)),
        ],
        compiler_params=pltpu.CompilerParams(
            collective_id=0, has_side_effects=True, vmem_limit_bytes=63 * 2**20
        ),
        cost_estimate=pl.CostEstimate(
            flops=2 * gauges * local * taps * columns,
            bytes_accessed=gauges * local * taps * 2,
            transcendentals=0,
        ),
    )(gauge_tiles, onsets, weights, active, rates, waveforms)
    return out.reshape(rows, scen, samples)


def solution(mesh):
    placed = (
        P(None, "src", None),
        P("groups", "src"),
        P("groups", "src"),
        P("groups", "src"),
        P("groups", "src", None),
        P("groups"),
    )
    return jax.shard_map(
        per_device, mesh=mesh, in_specs=placed, out_specs=P("src", "groups", None), check_vma=False
    )
```

```python
import functools

import jax
import jax.numpy as jnp
from jax import lax
from jax.experimental import pallas as pl
from jax.experimental.pallas import tpu as pltpu
from jax.sharding import PartitionSpec as P

GTILE = 128
MESH = pl.DeviceIdType.MESH
F32 = jnp.float32
BF16 = jnp.bfloat16


def column(block):
    size = block.shape[1]
    eye = lax.broadcasted_iota(jnp.int32, (size, size), 0) == lax.broadcasted_iota(
        jnp.int32, (size, size), 1
    )
    wide = jnp.broadcast_to(block.astype(F32), (size, size))
    return jnp.sum(jnp.where(eye, wide, 0.0), axis=1, keepdims=True)


def kernel(
    width, scen, samples, taps,
    tiles_hbm, onsets_hbm, weights_hbm, active_hbm, rates_hbm, w_hbm, out_ref,
    tiles_ref, onsets_ref, weights_ref, active_ref, rates_ref, small_sem,
    w_ref, scaled, moment, spread, lhs, keep,
    csend, crecv, ysend, yrecv, zsend, zrecv,
    ncs, ncr, nys, nyr, nzs, nzr,
    w_sem, cs_sem, cr_sem, ys_sem, yr_sem, zs_sem, zr_sem, n_ss, n_rs, nz_ss, nz_rs,
):
    line = width // 4
    steps = 2 * line
    rows = out_ref.shape[0]
    local = w_ref.shape[1]
    hist = rates_ref.shape[2]
    columns = scen * samples
    me = lax.axis_index("src")
    z = me // 4
    y = (me // 2) % 2
    core = me % 2
    mate = z * 4 + y * 2 + (1 - core)
    across = z * 4 + (1 - y) * 2 + core

    def stage(i):
        pair = (z // 2 + 1 + i // 2) % (line // 2)
        return pair * 2 + (z + 1 + i) % 2

    def target(i):
        near = z // 2 * 2 + (z + 1) % 2
        return (stage(i) * (i % 2) + near * (1 - i % 2)) * 4 + y * 2 + core

    def peer(j):
        return stage(j) * 4 + y * 2 + core

    small = [
        pltpu.make_async_copy(src, dst, small_sem.at[n])
        for n, (src, dst) in enumerate(
            (
                (rates_hbm, rates_ref),
                (onsets_hbm, onsets_ref),
                (weights_hbm, weights_ref),
                (active_hbm, active_ref),
                (tiles_hbm, tiles_ref),
            )
        )
    ]
    for copy in small:
        copy.start()
    load = pltpu.make_async_copy(w_hbm, w_ref, w_sem)
    load.start()

    barrier = pltpu.get_barrier_semaphore()
    for other in (mate, across):
        pl.semaphore_signal(barrier, inc=1, device_id={"src": other}, device_id_type=MESH)

    @pl.loop(0, line - 1)
    def _(j):
        pl.semaphore_signal(barrier, inc=1, device_id={"src": peer(j)}, device_id_type=MESH)

    def remote(src, dst, ss, rs, to):
        return pltpu.make_async_remote_copy(
            src_ref=src, dst_ref=dst, send_sem=ss, recv_sem=rs,
            device_id={"src": to}, device_id_type=MESH,
        )

    def ccopy(q):
        return remote(csend.at[q], crecv.at[q], cs_sem.at[q], cr_sem.at[q], mate)

    def ycopy(i):
        return remote(ysend.at[i], yrecv.at[i], ys_sem.at[i], yr_sem.at[i], across)

    def zcopy(j):
        return remote(zsend.at[j], zrecv.at[j], zs_sem.at[j], zr_sem.at[j], target(j // scen))

    def nzcopy(j):
        return remote(nzs, nzr.at[j], nz_ss.at[j], nz_rs.at[j], peer(j))

    nc = remote(ncs, ncr, n_ss.at[0], n_rs.at[0], mate)
    ny = remote(nys, nyr, n_ss.at[1], n_rs.at[1], across)

    for copy in small:
        copy.wait()
    amount = weights_ref[...] * active_ref[...]
    ncs[...] = jnp.broadcast_to(
        jnp.sum((1 + amount).astype(F32), axis=1, keepdims=True), ncs.shape
    )
    scaled[...] = jnp.zeros_like(scaled)
    index = lax.broadcasted_iota(jnp.int32, (local, hist), 1) - (taps - 1)
    for c in range(scen):
        amplitude = column((weights_ref[c : c + 1, :] * active_ref[c : c + 1, :]))
        onset = column(onsets_ref[c : c + 1, :])
        live = index.astype(F32) >= onset
        value = jnp.where(live, amplitude * rates_ref[c].astype(F32), 0.0)
        scaled[c, :, :hist] = value

    padded = scaled.shape[2]
    half = taps // 2

    @pl.loop(0, local)
    def _(s):
        for c in range(scen):
            row = jnp.broadcast_to(scaled[c, pl.ds(s, 1), :], (8, padded))
            eight = pltpu.roll(row, shift=padded - (half - 1), axis=1, stride=1, stride_axis=0)
            turned = jnp.concatenate(
                [eight] + [pltpu.roll(eight, shift=8 * n, axis=1) for n in range(1, half // 8)],
                axis=0,
            ).astype(BF16)
            base = pl.multiple_of(s * taps, taps)
            where = slice(c * samples, (c + 1) * samples)
            moment[pl.ds(base, half), where] = turned[:, half : half + samples]
            moment[pl.ds(pl.multiple_of(base + half, half), half), where] = turned[:, :samples]

    load.wait()
    pl.semaphore_wait(barrier, 2 + line - 1)
    nc.start()

    def compute(flip, i):
        q = flip * line + i
        zz = stage(i)
        yy = (1 - y) * (1 - flip) + y * flip
        for part in range(2):
            cc = (1 - core) * (1 - part) + core * part
            dest = (zz * 4 + yy * 2 + cc) * rows
            gauge = tiles_ref[dest // GTILE] * GTILE + dest % GTILE
            for n in range(taps // 128):
                block = w_ref[pl.ds(gauge, rows), :, n * 128 : (n + 1) * 128]
                spread[n] = block.astype(F32).reshape(rows * local, 128)
            for n in range(taps // 128):
                for s in range(local):
                    lhs[part * rows : (part + 1) * rows, s * taps + n * 128 : s * taps + (n + 1) * 128] = spread[
                        n, pl.ds(s, rows, stride=local), :
                    ].astype(BF16)

        for c in range(scen):
            k = q * scen + c

            @pl.loop(0, samples // 256)
            def _(n):
                cols = pl.ds(pl.multiple_of(n * 256, 256), 256)
                wide = pl.ds(pl.multiple_of(c * samples + n * 256, 256), 256)
                total = jnp.dot(lhs[...], moment[:, wide], preferred_element_type=F32)
                csend[k, :, cols] = total[:rows].astype(BF16)
                keep[k, :, cols] = total[rows:]

            ccopy(k).start()

    def first(i, c):
        k = i * scen + c
        ccopy(k).wait_recv()
        ysend[k] = (keep[k] + crecv[k].astype(F32)).astype(BF16)

        @pl.when(i > 0)
        def _():
            ycopy(k - scen).wait_send()

        ycopy(k).start()

    def summed(i, c):
        k = i * scen + c
        far = line * scen + k
        ccopy(far).wait_recv()
        ycopy(k).wait_recv()
        return keep[far] + crecv[far].astype(F32) + yrecv[k].astype(F32)

    def second(i, c):
        k = i * scen + c

        @pl.when(i % 2 == 0)
        def _():
            zsend[k] = summed(i, c).astype(BF16)

        @pl.when(i % 2 == 1)
        def _():
            zcopy(k - scen).wait_recv()
            zsend[k] = (summed(i, c) + zrecv[k - scen].astype(F32)).astype(BF16)

        zcopy(k).start()

    @pl.loop(0, steps + 2)
    def _(p):
        flip = p % 2
        i = p // 2 - flip

        @pl.when((i >= 0) & (i < line))
        def _():
            compute(flip, i)

        for c in range(scen):

            @pl.when((flip == 0) & (i >= 1))
            def _():
                first(i - 1, c)

            @pl.when((flip == 0) & (i >= 2))
            def _():
                second(i - 2, c)

        @pl.when((flip == 0) & (i == 1))
        def _():
            nc.wait()
            nys[...] = ncs[...] + ncr[...]
            ny.start()

        @pl.when((flip == 0) & (i == 2))
        def _():
            ny.wait()
            nzs[...] = nys[...] + nyr[...]

            @pl.loop(0, line - 1)
            def _(j):
                nzcopy(j).start()

    for c in range(scen):
        keep[c] = summed(line - 1, c)

    @pl.loop(0, line - 1)
    def _(j):
        nzcopy(j).wait_recv()

    def add_norm(j, norm):
        return norm + nzr[j]

    norm = lax.fori_loop(0, line - 1, add_norm, nzs[...])
    scale = jnp.full_like(norm, local * width) / norm

    @pl.loop(0, line // 2 - 1)
    def _(j):
        for c in range(scen):
            k = (2 * j + 1) * scen + c
            zcopy(k).wait_recv()
            keep[c] += zrecv[k].astype(F32)

    for c in range(scen):
        k = (line - 2) * scen + c
        zcopy(k).wait_recv()
        out_ref[:, c * samples : (c + 1) * samples] = (
            keep[c] + zrecv[k].astype(F32)
        ) * scale[c : c + 1, :1]

    @pl.loop(0, steps * scen)
    def _(q):
        ccopy(q).wait_send()

    for c in range(scen):
        ycopy((line - 1) * scen + c).wait_send()

    @pl.loop(0, (line - 1) * scen)
    def _(k):
        zcopy(k).wait_send()

    @pl.loop(0, line - 1)
    def _(j):
        nzcopy(j).wait_send()


def per_device(waveforms, onsets, weights, active, rates, gauge_tiles):
    gauges, local, taps = waveforms.shape
    scen, _, hist = rates.shape
    samples = hist - taps + 1
    width = lax.axis_size("src")
    line = width // 4
    rows = gauges // width
    columns = scen * samples
    vmem = pl.BlockSpec(memory_space=pltpu.VMEM)
    dma = pltpu.SemaphoreType.DMA
    out = pl.pallas_call(
        functools.partial(kernel, width, scen, samples, taps),
        out_shape=pltpu.VMEM((rows, columns), F32),
        in_specs=[pl.BlockSpec(memory_space=pltpu.HBM)] * 6,
        out_specs=vmem,
        scratch_shapes=[
            pltpu.SMEM(gauge_tiles.shape, jnp.int32),
            pltpu.VMEM(onsets.shape, jnp.int32),
            pltpu.VMEM(weights.shape, jnp.int32),
            pltpu.VMEM(active.shape, jnp.int32),
            pltpu.VMEM(rates.shape, BF16),
            dma((5,)),
            pltpu.VMEM((gauges, local, taps), BF16),
            pltpu.VMEM((scen, local, hist + 1), F32),
            pltpu.VMEM((local * taps, columns), BF16),
            pltpu.VMEM((taps // 128, rows * local, 128), F32),
            pltpu.VMEM((2 * rows, local * taps), BF16),
            pltpu.VMEM((2 * line * scen, rows, samples), F32),
            pltpu.VMEM((2 * line * scen, rows, samples), BF16),
            pltpu.VMEM((2 * line * scen, rows, samples), BF16),
            pltpu.VMEM((line * scen, rows, samples), BF16),
            pltpu.VMEM((line * scen, rows, samples), BF16),
            pltpu.VMEM(((line - 1) * scen, rows, samples), BF16),
            pltpu.VMEM(((line - 1) * scen, rows, samples), BF16),
            pltpu.VMEM((scen, 128), F32),
            pltpu.VMEM((scen, 128), F32),
            pltpu.VMEM((scen, 128), F32),
            pltpu.VMEM((scen, 128), F32),
            pltpu.VMEM((scen, 128), F32),
            pltpu.VMEM((line - 1, scen, 128), F32),
            dma,
            dma((2 * line * scen,)),
            dma((2 * line * scen,)),
            dma((line * scen,)),
            dma((line * scen,)),
            dma(((line - 1) * scen,)),
            dma(((line - 1) * scen,)),
            dma((2,)),
            dma((2,)),
            dma((line - 1,)),
            dma((line - 1,)),
        ],
        compiler_params=pltpu.CompilerParams(
            collective_id=0, has_side_effects=True, vmem_limit_bytes=63 * 2**20
        ),
        cost_estimate=pl.CostEstimate(
            flops=2 * gauges * local * taps * columns,
            bytes_accessed=gauges * local * taps * 2,
            transcendentals=0,
        ),
    )(gauge_tiles, onsets, weights, active, rates, waveforms)
    return out.reshape(rows, scen, samples)


def solution(mesh):
    placed = (
        P(None, "src", None),
        P("groups", "src"),
        P("groups", "src"),
        P("groups", "src"),
        P("groups", "src", None),
        P("groups"),
    )
    return jax.shard_map(
        per_device, mesh=mesh, in_specs=placed, out_specs=P("src", "groups", None), check_vma=False
    )
```

```python
import functools

import jax
import jax.numpy as jnp
from jax import lax
from jax.experimental import pallas as pl
from jax.experimental.pallas import tpu as pltpu
from jax.sharding import PartitionSpec as P

GTILE = 128
MESH = pl.DeviceIdType.MESH
F32 = jnp.float32
BF16 = jnp.bfloat16


def column(block):
    size = block.shape[1]
    eye = lax.broadcasted_iota(jnp.int32, (size, size), 0) == lax.broadcasted_iota(
        jnp.int32, (size, size), 1
    )
    wide = jnp.broadcast_to(block.astype(F32), (size, size))
    return jnp.sum(jnp.where(eye, wide, 0.0), axis=1, keepdims=True)


def kernel(
    width, scen, samples, taps,
    tiles_hbm, onsets_hbm, weights_hbm, active_hbm, rates_hbm, w_hbm, out_ref,
    tiles_ref, onsets_ref, weights_ref, active_ref, rates_ref, small_sem,
    w_ref, scaled, moment, spread, lhs, keep,
    csend, crecv, ysend, yrecv, zsend, zrecv,
    ncs, ncr, nys, nyr, nzs, nzr,
    w_sem, cs_sem, cr_sem, ys_sem, yr_sem, zs_sem, zr_sem, n_ss, n_rs, nz_ss, nz_rs,
):
    line = width // 4
    steps = 2 * line
    rows = out_ref.shape[0]
    local = w_ref.shape[1]
    hist = rates_ref.shape[2]
    columns = scen * samples
    me = lax.axis_index("src")
    z = me // 4
    y = (me // 2) % 2
    core = me % 2
    mate = z * 4 + y * 2 + (1 - core)
    across = z * 4 + (1 - y) * 2 + core

    def stage(i):
        pair = (z // 2 + 1 + i // 2) % (line // 2)
        return pair * 2 + (z + 1 + i) % 2

    def target(i):
        near = z // 2 * 2 + (z + 1) % 2
        return (stage(i) * (i % 2) + near * (1 - i % 2)) * 4 + y * 2 + core

    def peer(j):
        return stage(j) * 4 + y * 2 + core

    small = [
        pltpu.make_async_copy(src, dst, small_sem.at[n])
        for n, (src, dst) in enumerate(
            (
                (rates_hbm, rates_ref),
                (onsets_hbm, onsets_ref),
                (weights_hbm, weights_ref),
                (active_hbm, active_ref),
                (tiles_hbm, tiles_ref),
            )
        )
    ]
    for copy in small:
        copy.start()
    load = pltpu.make_async_copy(w_hbm, w_ref, w_sem)
    load.start()

    barrier = pltpu.get_barrier_semaphore()
    for other in (mate, across):
        pl.semaphore_signal(barrier, inc=1, device_id={"src": other}, device_id_type=MESH)

    @pl.loop(0, line - 1)
    def _(j):
        pl.semaphore_signal(barrier, inc=1, device_id={"src": peer(j)}, device_id_type=MESH)

    def remote(src, dst, ss, rs, to):
        return pltpu.make_async_remote_copy(
            src_ref=src, dst_ref=dst, send_sem=ss, recv_sem=rs,
            device_id={"src": to}, device_id_type=MESH,
        )

    def ccopy(q):
        return remote(csend.at[q], crecv.at[q], cs_sem.at[q], cr_sem.at[q], mate)

    def ycopy(i):
        return remote(ysend.at[i], yrecv.at[i], ys_sem.at[i], yr_sem.at[i], across)

    def zcopy(j):
        return remote(zsend.at[j], zrecv.at[j], zs_sem.at[j], zr_sem.at[j], target(j // scen))

    def nzcopy(j):
        return remote(nzs, nzr.at[j], nz_ss.at[j], nz_rs.at[j], peer(j))

    nc = remote(ncs, ncr, n_ss.at[0], n_rs.at[0], mate)
    ny = remote(nys, nyr, n_ss.at[1], n_rs.at[1], across)

    for copy in small:
        copy.wait()
    amount = weights_ref[...] * active_ref[...]
    ncs[...] = jnp.broadcast_to(
        jnp.sum((1 + amount).astype(F32), axis=1, keepdims=True), ncs.shape
    )
    scaled[...] = jnp.zeros_like(scaled)
    index = lax.broadcasted_iota(jnp.int32, (local, hist), 1) - (taps - 1)
    for c in range(scen):
        amplitude = column((weights_ref[c : c + 1, :] * active_ref[c : c + 1, :]))
        onset = column(onsets_ref[c : c + 1, :])
        live = index.astype(F32) >= onset
        value = jnp.where(live, amplitude * rates_ref[c].astype(F32), 0.0)
        scaled[c, :, :hist] = value

    padded = scaled.shape[2]
    half = taps // 2

    @pl.loop(0, local)
    def _(s):
        for c in range(scen):
            row = jnp.broadcast_to(scaled[c, pl.ds(s, 1), :], (8, padded))
            eight = pltpu.roll(row, shift=padded - (half - 1), axis=1, stride=1, stride_axis=0)
            turned = jnp.concatenate(
                [eight] + [pltpu.roll(eight, shift=8 * n, axis=1) for n in range(1, half // 8)],
                axis=0,
            ).astype(BF16)
            base = pl.multiple_of(s * taps, taps)
            where = slice(c * samples, (c + 1) * samples)
            moment[pl.ds(base, half), where] = turned[:, half : half + samples]
            moment[pl.ds(pl.multiple_of(base + half, half), half), where] = turned[:, :samples]

    load.wait()
    pl.semaphore_wait(barrier, 2 + line - 1)
    nc.start()

    def compute(flip, i):
        q = flip * line + i
        zz = stage(i)
        yy = (1 - y) * (1 - flip) + y * flip
        for part in range(2):
            cc = (1 - core) * (1 - part) + core * part
            dest = (zz * 4 + yy * 2 + cc) * rows
            gauge = tiles_ref[dest // GTILE] * GTILE + dest % GTILE
            for n in range(taps // 128):
                block = w_ref[pl.ds(gauge, rows), :, n * 128 : (n + 1) * 128]
                spread[n] = block.astype(F32).reshape(rows * local, 128)
            for n in range(taps // 128):
                for s in range(local):
                    lhs[part * rows : (part + 1) * rows, s * taps + n * 128 : s * taps + (n + 1) * 128] = spread[
                        n, pl.ds(s, rows, stride=local), :
                    ].astype(BF16)

        for c in range(scen):
            k = q * scen + c

            @pl.loop(0, samples // 256, unroll=True)
            def _(n):
                cols = pl.ds(pl.multiple_of(n * 256, 256), 256)
                wide = pl.ds(pl.multiple_of(c * samples + n * 256, 256), 256)
                total = jnp.dot(lhs[...], moment[:, wide], preferred_element_type=F32)
                csend[k, :, cols] = total[:rows].astype(BF16)
                keep[k, :, cols] = total[rows:]

            ccopy(k).start()

    def first(i, c):
        k = i * scen + c
        ccopy(k).wait_recv()
        ysend[k] = (keep[k] + crecv[k].astype(F32)).astype(BF16)

        @pl.when(i > 0)
        def _():
            ycopy(k - scen).wait_send()

        ycopy(k).start()

    def summed(i, c):
        k = i * scen + c
        far = line * scen + k
        ccopy(far).wait_recv()
        ycopy(k).wait_recv()
        return keep[far] + crecv[far].astype(F32) + yrecv[k].astype(F32)

    def second(i, c):
        k = i * scen + c

        @pl.when(i % 2 == 0)
        def _():
            zsend[k] = summed(i, c).astype(BF16)

        @pl.when(i % 2 == 1)
        def _():
            zcopy(k - scen).wait_recv()
            zsend[k] = (summed(i, c) + zrecv[k - scen].astype(F32)).astype(BF16)

        zcopy(k).start()

    @pl.loop(0, steps + 2)
    def _(p):
        flip = p % 2
        i = p // 2 - flip

        @pl.when((i >= 0) & (i < line))
        def _():
            compute(flip, i)

        for c in range(scen):

            @pl.when((flip == 0) & (i >= 1))
            def _():
                first(i - 1, c)

            @pl.when((flip == 0) & (i >= 2))
            def _():
                second(i - 2, c)

        @pl.when((flip == 0) & (i == 1))
        def _():
            nc.wait()
            nys[...] = ncs[...] + ncr[...]
            ny.start()

        @pl.when((flip == 0) & (i == 2))
        def _():
            ny.wait()
            nzs[...] = nys[...] + nyr[...]

            @pl.loop(0, line - 1)
            def _(j):
                nzcopy(j).start()

    for c in range(scen):
        keep[c] = summed(line - 1, c)

    @pl.loop(0, line - 1)
    def _(j):
        nzcopy(j).wait_recv()

    def add_norm(j, norm):
        return norm + nzr[j]

    norm = lax.fori_loop(0, line - 1, add_norm, nzs[...])
    scale = jnp.full_like(norm, local * width) / norm

    @pl.loop(0, line // 2 - 1)
    def _(j):
        for c in range(scen):
            k = (2 * j + 1) * scen + c
            zcopy(k).wait_recv()
            keep[c] += zrecv[k].astype(F32)

    for c in range(scen):
        k = (line - 2) * scen + c
        zcopy(k).wait_recv()
        out_ref[:, c * samples : (c + 1) * samples] = (
            keep[c] + zrecv[k].astype(F32)
        ) * scale[c : c + 1, :1]

    @pl.loop(0, steps * scen)
    def _(q):
        ccopy(q).wait_send()

    for c in range(scen):
        ycopy((line - 1) * scen + c).wait_send()

    @pl.loop(0, (line - 1) * scen)
    def _(k):
        zcopy(k).wait_send()

    @pl.loop(0, line - 1)
    def _(j):
        nzcopy(j).wait_send()


def per_device(waveforms, onsets, weights, active, rates, gauge_tiles):
    gauges, local, taps = waveforms.shape
    scen, _, hist = rates.shape
    samples = hist - taps + 1
    width = lax.axis_size("src")
    line = width // 4
    rows = gauges // width
    columns = scen * samples
    vmem = pl.BlockSpec(memory_space=pltpu.VMEM)
    dma = pltpu.SemaphoreType.DMA
    out = pl.pallas_call(
        functools.partial(kernel, width, scen, samples, taps),
        out_shape=pltpu.VMEM((rows, columns), F32),
        in_specs=[pl.BlockSpec(memory_space=pltpu.HBM)] * 6,
        out_specs=vmem,
        scratch_shapes=[
            pltpu.SMEM(gauge_tiles.shape, jnp.int32),
            pltpu.VMEM(onsets.shape, jnp.int32),
            pltpu.VMEM(weights.shape, jnp.int32),
            pltpu.VMEM(active.shape, jnp.int32),
            pltpu.VMEM(rates.shape, BF16),
            dma((5,)),
            pltpu.VMEM((gauges, local, taps), BF16),
            pltpu.VMEM((scen, local, hist + 1), F32),
            pltpu.VMEM((local * taps, columns), BF16),
            pltpu.VMEM((taps // 128, rows * local, 128), F32),
            pltpu.VMEM((2 * rows, local * taps), BF16),
            pltpu.VMEM((2 * line * scen, rows, samples), F32),
            pltpu.VMEM((2 * line * scen, rows, samples), BF16),
            pltpu.VMEM((2 * line * scen, rows, samples), BF16),
            pltpu.VMEM((line * scen, rows, samples), BF16),
            pltpu.VMEM((line * scen, rows, samples), BF16),
            pltpu.VMEM(((line - 1) * scen, rows, samples), BF16),
            pltpu.VMEM(((line - 1) * scen, rows, samples), BF16),
            pltpu.VMEM((scen, 128), F32),
            pltpu.VMEM((scen, 128), F32),
            pltpu.VMEM((scen, 128), F32),
            pltpu.VMEM((scen, 128), F32),
            pltpu.VMEM((scen, 128), F32),
            pltpu.VMEM((line - 1, scen, 128), F32),
            dma,
            dma((2 * line * scen,)),
            dma((2 * line * scen,)),
            dma((line * scen,)),
            dma((line * scen,)),
            dma(((line - 1) * scen,)),
            dma(((line - 1) * scen,)),
            dma((2,)),
            dma((2,)),
            dma((line - 1,)),
            dma((line - 1,)),
        ],
        compiler_params=pltpu.CompilerParams(
            collective_id=0, has_side_effects=True, vmem_limit_bytes=63 * 2**20
        ),
        cost_estimate=pl.CostEstimate(
            flops=2 * gauges * local * taps * columns,
            bytes_accessed=gauges * local * taps * 2,
            transcendentals=0,
        ),
    )(gauge_tiles, onsets, weights, active, rates, waveforms)
    return out.reshape(rows, scen, samples)


def solution(mesh):
    placed = (
        P(None, "src", None),
        P("groups", "src"),
        P("groups", "src"),
        P("groups", "src"),
        P("groups", "src", None),
        P("groups"),
    )
    return jax.shard_map(
        per_device, mesh=mesh, in_specs=placed, out_specs=P("src", "groups", None), check_vma=False
    )
```
